512 devices in a mesh: leaf: 128 (over z, y, core), lvl: 4 (over x).
Axes of the slice: x: 4, y: 8, z: 8, core: 2. Of those that a mesh axis runs over, the one named last changes fastest.
Arguments:
- charges: bfloat16 [8192, 512], P('leaf', 'lvl'), may hold values from -6 to 6
- p2m_matrix: bfloat16 [512, 512], P('lvl'), may hold values from -0.25 to 0.25
- m2m_matrices: bfloat16 [8, 512, 512], P(None, None, 'lvl'), may hold values from -0.09375 to 0.09375
- leaf_ops: bfloat16 [8, 512, 512], P(None, None, 'lvl'), may hold values from -0.0546875 to 0.0546875
- coarse_ops: bfloat16 [4, 512, 512], P(None, None, 'lvl'), may hold values from -0.0546875 to 0.0546875
- l2l_matrices: bfloat16 [8, 512, 512], P(None, None, 'lvl'), may hold values from -0.25 to 0.25
- l2p_matrix: bfloat16 [512, 512], replicated, may hold values from -0.25 to 0.25
- near_kernel_tiles: bfloat16 [4, 512, 512], P(None, None, 'lvl'), may hold values from -0.09375 to 0.09375
- send_rows: int32 [128, 128, 4], P('leaf'), may hold values from 0 to 63
- m2l_src: int32 [8192, 24], P('leaf'), may hold values from 0 to 575, as said below
- m2l_op: int32 [8192, 24], P('leaf'), may hold values from 0 to 7
- m2l_count: int32 [8192], P('leaf'), may hold values from 12 to 24
- coarse_src: int32 [1024, 24], P('leaf'), may hold values from 0 to 1023
- coarse_op: int32 [1024, 24], P('leaf'), may hold values from 0 to 3
- near_src: int32 [8192, 8], P('leaf'), may hold values from 0 to 8191, as said below
- neighbour_kernel_type: int32 [8192, 8], P('leaf'), may hold values from 0 to 3
Outputs:
- potential: float32 [8192, 512], P('leaf', 'lvl')
The draws below stay inside these ranges and needn't reach their ends.
Inputs may be any that keep to these rules, and one draw needn't show every extreme that they name: `send_rows`: a local leaf index of the sending device. `m2l_src`: an index into pool_d of the leaf's block; on each block every one of the 576 entries is named in some slot below 12. `near_src`: a neighbour lies within 32 leaves of its target in Morton order.
All inputs are finite; a program needn't handle non-finite values.
Results may differ from the reference program's by a relative error of at most 0.018.
Values may be sent and summed in bfloat16 or wider, within the bound.
A program may use at most 64 MiB of HBM per device.

```python
import jax
import jax.numpy as jnp
from jax import lax

K = 512
LEAF_UNKNOWNS = 512
LEAF_DEV = 64
CAP = 4
SLOTS = 24
CSLOTS = 24
NEIGHBOUR_COUNT = 8
NOPS = 8
CNOPS = 4
NEAR_KINDS = 4
LEAF_DEVICES = 128
LEAF_TOTAL = 8192
NC = 1024
POOL = 576
MAX_CODE_SPAN = 32
N_LEAF = 128


def draw_m2l_src(key, part):
    key = jax.random.fold_in(key, 7)
    blocks = LEAF_TOTAL // LEAF_DEV
    half = SLOTS // 2
    keys = jax.random.split(key, blocks + 1)

    def cover(block_key):
        order = jax.random.permutation(block_key, LEAF_DEV * half)
        return (order % POOL).reshape(LEAF_DEV, half)
    first = jax.vmap(cover)(keys[:blocks]).reshape(LEAF_TOTAL, half)
    others = jax.random.randint(keys[blocks], (LEAF_TOTAL, SLOTS - half), 0, POOL)
    return jnp.concatenate([first, others], 1).astype(jnp.int32)


def draw_near_src(key, part):
    key = jax.random.fold_in(key, 11)
    position = jnp.arange(LEAF_TOTAL, dtype=jnp.int32)[:, None]
    code_shift = jax.random.randint(key, (LEAF_TOTAL, NEIGHBOUR_COUNT), -MAX_CODE_SPAN, MAX_CODE_SPAN + 1)
    source = position + code_shift
    outside = (source < 0) | (source >= LEAF_TOTAL)
    return jnp.where(outside, position - code_shift, source).astype(jnp.int32)


def touch_ends(drawn, key, least, high):
    longest = drawn.shape.index(max(drawn.shape))
    spots = []
    for shift in (0, 1):
        where = [jax.random.randint(jax.random.fold_in(key, axis), (), 0, length) for axis, length in enumerate(drawn.shape)]
        where[longest] = (where[longest] + shift) % drawn.shape[longest]
        spots.append(tuple(where))
    return drawn.at[spots[0]].set(least).at[spots[1]].set(high)


def block_scale(own_key, shape, cuts, smallest, largest):
    factor_of, own = 1.0, jax.random.fold_in(own_key, 6)
    for axis_at, parts in cuts:
        draws = jnp.exp(jax.random.uniform(jax.random.fold_in(own, axis_at), (parts,), jnp.float32, smallest / len(cuts), largest / len(cuts)))
        factor_of = factor_of * jnp.repeat(draws, shape[axis_at] // parts).reshape([-1 if axis == axis_at else 1 for axis in range(len(shape))])
    return factor_of


def gaussian(stream_key, shape, spread, reach, cuts=(), held_as=jnp.bfloat16):
    result = jax.random.normal(stream_key, shape, jnp.float32) * spread
    if len(cuts) > 0:
        result = block_scale(stream_key, shape, cuts, -0.22, 0.18) * result
    return jnp.clip(result, min=-reach, max=reach).astype(held_as)


def setup_inputs(seed: int = 0) -> dict:
    key_of = jax.random.split(jax.random.key(seed), 17)
    return {
        "charges": gaussian(key_of[0], (LEAF_TOTAL, LEAF_UNKNOWNS), 1.0, 6.0, ((0, 128), (1, 4))),
        "p2m_matrix": gaussian(key_of[1], (LEAF_UNKNOWNS, K), LEAF_UNKNOWNS ** -0.5, 0.25, ((0, 4),)),
        "m2m_matrices": gaussian(key_of[2], (8, K, K), (8 * K) ** -0.5, 0.09375, ((2, 4),)),
        "leaf_ops": gaussian(key_of[3], (NOPS, K, K), (K * SLOTS) ** -0.5, 0.0546875, ((2, 4),)),
        "coarse_ops": gaussian(key_of[4], (CNOPS, K, K), (K * CSLOTS) ** -0.5, 0.0546875, ((2, 4),)),
        "l2l_matrices": gaussian(key_of[5], (8, K, K), K ** -0.5, 0.25, ((2, 4),)),
        "l2p_matrix": gaussian(key_of[6], (K, LEAF_UNKNOWNS), K ** -0.5, 0.25),
        "near_kernel_tiles": gaussian(key_of[7], (NEAR_KINDS, LEAF_UNKNOWNS, LEAF_UNKNOWNS), (LEAF_UNKNOWNS * NEIGHBOUR_COUNT) ** -0.5, 0.09375, ((2, 4),)),
        "send_rows": touch_ends(jax.random.randint(key_of[8], (LEAF_DEVICES, LEAF_DEVICES, CAP), 0, LEAF_DEV), jax.random.fold_in(key_of[8], 1), 0, LEAF_DEV - 1).astype(jnp.int32),
        "m2l_src": draw_m2l_src(jax.random.fold_in(key_of[16], 71), 0),
        "m2l_op": touch_ends(jax.random.randint(key_of[10], (LEAF_TOTAL, SLOTS), 0, NOPS), jax.random.fold_in(key_of[10], 1), 0, NOPS - 1).astype(jnp.int32),
        "m2l_count": touch_ends(jax.random.randint(key_of[11], (LEAF_TOTAL,), SLOTS // 2, SLOTS + 1), jax.random.fold_in(key_of[11], 1), SLOTS // 2, SLOTS).astype(jnp.int32),
        "coarse_src": touch_ends(jax.random.randint(key_of[12], (NC, CSLOTS), 0, NC), jax.random.fold_in(key_of[12], 1), 0, NC - 1).astype(jnp.int32),
        "coarse_op": touch_ends(jax.random.randint(key_of[13], (NC, CSLOTS), 0, CNOPS), jax.random.fold_in(key_of[13], 1), 0, CNOPS - 1).astype(jnp.int32),
        "near_src": draw_near_src(jax.random.fold_in(key_of[16], 71), 0),
        "neighbour_kernel_type": touch_ends(jax.random.randint(key_of[15], (LEAF_TOTAL, NEIGHBOUR_COUNT), 0, NEAR_KINDS), jax.random.fold_in(key_of[15], 1), 0, NEAR_KINDS - 1).astype(jnp.int32),
    }


def reference(charges, p2m_matrix, m2m_matrices, leaf_ops, coarse_ops, l2l_matrices, l2p_matrix, near_kernel_tiles, send_rows, m2l_src, m2l_op, m2l_count, coarse_src, coarse_op, near_src, neighbour_kernel_type):
    moments = jnp.dot(charges, p2m_matrix, preferred_element_type=jnp.float32).astype(jnp.bfloat16)
    children = moments.reshape(NC, 8, K).astype(jnp.float32)
    parents = jnp.einsum('cok,okj->cj', children, m2m_matrices.astype(jnp.float32)).astype(jnp.bfloat16)
    coarse_table = jnp.einsum('ck,tkj->tcj', parents.astype(jnp.float32), coarse_ops.astype(jnp.float32))
    coarse_acc = jnp.zeros((NC, K), jnp.float32)
    for neighbour_position in range(CSLOTS):
        coarse_acc = coarse_acc + coarse_table[coarse_op[:, neighbour_position], coarse_src[:, neighbour_position]]
    coarse_local = coarse_acc.astype(jnp.bfloat16)
    ops_wide = leaf_ops.astype(jnp.float32)

    def leaf_block(block):
        own = lax.dynamic_slice_in_dim(moments, block * LEAF_DEV, LEAF_DEV, 0)
        sent = lax.dynamic_index_in_dim(send_rows, block, 1, keepdims=False)
        rows = (jnp.arange(N_LEAF, dtype=jnp.int32)[:, None] * LEAF_DEV + sent).reshape(-1)
        pool = jnp.concatenate([own, moments[rows]], 0).astype(jnp.float32)
        table = jnp.einsum('pk,tkj->tpj', pool, ops_wide)
        sources = lax.dynamic_slice_in_dim(m2l_src, block * LEAF_DEV, LEAF_DEV, 0)
        operators = lax.dynamic_slice_in_dim(m2l_op, block * LEAF_DEV, LEAF_DEV, 0)
        counts = lax.dynamic_slice_in_dim(m2l_count, block * LEAF_DEV, LEAF_DEV, 0)
        picked = table[operators, sources]
        live = jnp.arange(SLOTS, dtype=jnp.int32)[None, :] < counts[:, None]
        return jnp.sum(jnp.where(live[:, :, None], picked, 0.0), axis=1)

    leaf_far = lax.map(leaf_block, jnp.arange(N_LEAF, dtype=jnp.int32)).reshape(LEAF_TOTAL, K)
    down = jnp.einsum('ck,okj->coj', coarse_local.astype(jnp.float32), l2l_matrices.astype(jnp.float32)).reshape(LEAF_TOTAL, K)
    local = (leaf_far + down).astype(jnp.bfloat16)
    far = jnp.dot(local, l2p_matrix, preferred_element_type=jnp.float32)
    near = jnp.zeros((LEAF_TOTAL, LEAF_UNKNOWNS), jnp.float32)
    for kind in range(NEAR_KINDS):
        tile_out = jnp.dot(charges, near_kernel_tiles[kind], preferred_element_type=jnp.float32)
        for neighbour_position in range(NEIGHBOUR_COUNT):
            near = near + jnp.where((neighbour_kernel_type[:, neighbour_position] == kind)[:, None], tile_out[near_src[:, neighbour_position]], 0.0)
    return far + near
```

```python
import jax
import jax.numpy as jnp
from jax import lax
from jax.experimental import pallas as pl
from jax.experimental.pallas import tpu as pltpu
from jax.sharding import PartitionSpec as P

MESH = pl.DeviceIdType.MESH
BF16 = jnp.bfloat16
F32 = jnp.float32
I32 = jnp.int32
XOFF = (2, 1, 3)


def mm(a, b):
    return jnp.dot(a, b, preferred_element_type=F32)


def mm_nt(a, b):
    return lax.dot_general(a, b, (((1,), (1,)), ((), ())), preferred_element_type=F32)


def iota(shape, dim):
    return lax.broadcasted_iota(I32, shape, dim)


def flipped(code):
    slots, leaves = code.shape
    halves = jnp.concatenate([code >> 6, code & 63], axis=0).astype(F32).astype(BF16)
    eye = (iota((leaves, leaves), 0) == iota((leaves, leaves), 1)).astype(F32).astype(BF16)
    turned = mm_nt(eye, halves)
    return (turned[:, :slots] * 64.0 + turned[:, slots:]).astype(I32)


def counts(code, width, start):
    rows, slots = code.shape
    columns = iota((rows, width), 1)
    code = code - start
    total = jnp.zeros((rows, width), F32)
    for s in range(slots):
        total = total + jnp.where(code[:, s : s + 1] == columns, 1.0, 0.0)
    return total.astype(BF16)


def kernel(
    charges_h, p2m_h, m2m_h, lops_h, cops_h, l2l_h, l2p_h, tiles_h,
    send_h, src_h, op_h, count_h, csrc_h, cop_h, near_h, kind_h,
    out_ref,
    charges, p2m, m2m, l2l, l2p, tiles,
    send, src, op, count, csrc, cop, near_v, kind_v,
    load_sem,
    mom32, mom4, mpart, mslot, ext, leafw, coarsew,
    pick, s_leaf, s_coarse, s_near,
    msg, rbuf, cbuf, pool, gsum,
    coarse_own, coarse_slot, down, leafpot, pot, pot_out, pot_slot,
    mp_s, mp_r, ch_s, ch_r, lw_s, lw_r, cw_s, cw_r, own_w, sw_s, sw_r,
    halo_s, halo_r, far_s, far_r, sib_s, sib_r, co_s, co_r, po_s, po_r,
    ready,
):
    leaf = lax.axis_index("leaf")
    lvl = lax.axis_index("lvl")
    core = lax.rem(leaf, 2)
    chip = lax.div(leaf, 2)
    z = lax.div(leaf, 16)
    y = lax.rem(chip, 8)
    other = 1 - core
    sibling = (chip * 2 + other, lvl)
    right = (lax.rem(leaf + 1, 128), lvl)
    left = (lax.rem(leaf + 127, 128), lvl)
    beside = (lax.rem(leaf + 127 + 2 * core, 128), lvl)
    near_far = (4, 3, 5, 2, 6, 1, 7)
    zpeers = [(lax.rem(z + k, 8) * 16 + y * 2 + core, lvl) for k in near_far]
    ypeers = [(z * 16 + lax.rem(y + k, 8) * 2 + core, lvl) for k in near_far]
    xpeers = [(leaf, lax.rem(lvl + k, 4)) for k in XOFF]
    mine = pl.ds(pl.multiple_of(lvl * 128, 128), 128)

    barrier = pltpu.get_barrier_semaphore()
    greeted = zpeers + ypeers + xpeers + [sibling, beside]
    for peer in greeted:
        pl.semaphore_signal(barrier, inc=1, device_id=peer, device_id_type=MESH)

    loads = {}
    pairs = (
        ("charges", charges_h, charges), ("p2m", p2m_h, p2m), ("send", send_h, send),
        ("csrc", csrc_h, csrc), ("cop", cop_h, cop), ("near", near_h, near_v), ("kind", kind_h, kind_v),
        ("src", src_h, src), ("op", op_h, op), ("count", count_h, count),
        ("m2m", m2m_h, m2m), ("tiles", tiles_h, tiles), ("l2l", l2l_h, l2l), ("l2p", l2p_h, l2p),
    )
    for i, (name, source, target) in enumerate(pairs):
        loads[name] = pltpu.make_async_copy(source, target, load_sem.at[i])
        loads[name].start()

    def remote(source, target, send_sem, recv_sem, peer):
        copy = pltpu.make_async_remote_copy(
            src_ref=source, dst_ref=target, send_sem=send_sem, recv_sem=recv_sem,
            device_id=peer, device_id_type=MESH,
        )
        copy.start()
        return copy

    loads["charges"].wait()
    loads["p2m"].wait()
    partial = mm(charges[...], p2m[...])
    mom32[...] = partial
    mpart[...] = partial.astype(BF16)
    ext[32:96, mine] = charges[...]

    loads["send"].wait()
    row = iota((512, 128), 0)
    dest = (row >> 3) * 2 + jnp.where(((row >> 2) & 1) == 0, core, other)
    spread = (dest == iota((512, 128), 1)).astype(F32).astype(BF16)
    chosen = mm_nt(spread, send[...].astype(F32).astype(BF16))
    slot = iota((512, 4), 1) == (iota((512, 4), 0) & 3)
    chosen = jnp.sum(jnp.where(slot, chosen, 0.0), axis=1, keepdims=True).astype(I32)
    pick[...] = (chosen == iota((512, 64), 1)).astype(F32).astype(BF16)

    loads["csrc"].wait()
    loads["cop"].wait()
    cv = csrc[...]
    cpos = (cv & ~15) + (cv & 7) + jnp.where(((cv >> 3) & 1) == core, 0, 1024)
    ctag = cop[...]
    ccode = jnp.concatenate([jnp.where(ctag == t, cpos, -1) for t in range(4)], axis=0)
    for part in range(4):
        s_coarse[:, part * 512 : (part + 1) * 512] = counts(ccode, 512, part * 512)

    loads["near"].wait()
    loads["kind"].wait()
    ncode = kind_v[...] * 128 + (near_v[...] - (leaf * 64 - 32))
    s_near[...] = counts(flipped(ncode), 512, 0)

    pl.semaphore_wait(barrier, len(greeted))

    mp = [remote(mpart, mslot.at[i], mp_s.at[i], mp_r.at[i], xpeers[i]) for i in range(3)]
    ch = [
        remote(charges, ext.at[pl.ds(32, 64), mine], ch_s.at[i], ch_r.at[i], xpeers[i])
        for i in range(3)
    ]
    for peer in ypeers:
        pl.semaphore_signal(ready, inc=1, device_id=peer, device_id_type=MESH)

    loads["src"].wait()
    loads["op"].wait()
    loads["count"].wait()
    sv = src[...]
    w = sv - 64
    sent = 64 + ((w >> 3) << 2) + (w & 3) + jnp.where(((w >> 2) & 1) == core, 0, 256)
    spos = jnp.where(sv < 64, sv, sent)
    scode = jnp.where(iota((24, 64), 0) < count[...], op[...] * 640 + spos, -1)
    scode = flipped(scode)

    def fill(t, carry):
        s_leaf[:, pl.ds(pl.multiple_of(t * 640, 128), 640)] = counts(scode, 640, t * 640)
        return carry

    lax.fori_loop(0, 8, fill, 0)

    for copy in mp:
        copy.wait_recv()
    moments = mom32[...]
    for i in range(3):
        moments = moments + mslot[i].astype(F32)
    moments = moments.astype(BF16).astype(F32)
    for j in range(4):
        mom4[j] = moments[:, j * 128 : (j + 1) * 128]

    chalf = pl.ds(core * 2, 2)
    lhalf = pl.ds(core * 4, 4)
    cw, lw = [], []
    for i, k in enumerate(XOFF):
        rows = pl.ds(pl.multiple_of(lax.rem(lvl + k, 4) * 128, 128), 128)
        cw.append(remote(cops_h.at[chalf, rows], coarsew.at[chalf, :, mine], cw_s.at[i], cw_r.at[i], xpeers[i]))
    for i, k in enumerate(XOFF):
        rows = pl.ds(pl.multiple_of(lax.rem(lvl + k, 4) * 128, 128), 128)
        lw.append(remote(lops_h.at[lhalf, rows], leafw.at[lhalf, :, mine], lw_s.at[i], lw_r.at[i], xpeers[i]))
    own_c = pltpu.make_async_copy(cops_h.at[chalf, mine], coarsew.at[chalf, :, mine], own_w.at[0])
    own_l = pltpu.make_async_copy(lops_h.at[lhalf, mine], leafw.at[lhalf, :, mine], own_w.at[1])
    own_c.start()
    own_l.start()

    loads["m2m"].wait()
    parents = jnp.zeros((8, 128), F32)
    for o in range(8):
        octant = [mom4[j, pl.ds(o, 8, stride=8), :] for j in range(4)]
        parents = parents + mm(jnp.concatenate(octant, axis=1).astype(BF16), m2m[o])
    quarter = mom4[lvl].astype(BF16)
    chosen_rows = mm(pick[...], quarter).reshape(64, 8, 128)
    both = jnp.concatenate([jnp.broadcast_to(parents[None], (64, 8, 128)), chosen_rows], axis=1)
    msg[...] = both.astype(BF16)

    pl.semaphore_wait(ready, 7)

    def offset(t):
        return 4 + (1 - 2 * lax.rem(t, 2)) * lax.div(t + 1, 2)

    def send_one(i, carry):
        pz = lax.rem(z + offset(lax.div(i, 8)), 8)
        py = lax.rem(y + offset(lax.rem(i, 8)), 8)
        there = pz * 8 + py
        pltpu.make_async_remote_copy(
            src_ref=msg.at[there], dst_ref=rbuf.at[chip], send_sem=far_s, recv_sem=far_r,
            device_id=(there * 2 + core, lvl), device_id_type=MESH,
        ).start()
        return carry

    lax.fori_loop(0, 63, send_one, 0)
    rbuf[pl.ds(chip, 1)] = msg[pl.ds(chip, 1)]
    pool[0:64, :] = quarter
    pool[576:640, :] = jnp.zeros((64, 128), BF16)

    for copy in ch:
        copy.wait_recv()
    halo = [
        remote(ext.at[pl.ds(64, 32)], ext.at[pl.ds(0, 32)], halo_s.at[0], halo_r.at[0], right),
        remote(ext.at[pl.ds(32, 32)], ext.at[pl.ds(96, 32)], halo_s.at[1], halo_r.at[1], left),
    ]

    own_c.wait()
    for copy in cw:
        copy.wait_recv()
    swap = [remote(coarsew.at[chalf], coarsew.at[chalf], sw_s.at[0], sw_r.at[0], sibling)]

    for copy in halo:
        copy.wait_recv()
    loads["tiles"].wait()
    close = jnp.zeros((64, 128), F32)
    for t in range(4):
        close = close + mm(s_near[:, t * 128 : (t + 1) * 128], mm(ext[...], tiles[t]).astype(BF16))
    out_ref[...] = close

    own_l.wait()
    for copy in lw:
        copy.wait_recv()
    swap.append(remote(leafw.at[lhalf], leafw.at[lhalf], sw_s.at[1], sw_r.at[1], sibling))

    pltpu.make_async_copy(msg.at[pl.ds(0, 63)], rbuf.at[pl.ds(0, 63)], far_r).wait()
    sib = remote(rbuf, cbuf, sib_s, sib_r, sibling)
    gathered = mm(s_coarse[:, :1024], rbuf[...].reshape(1024, 128))

    def swapped(x):
        return jnp.concatenate([x[:, 4:], x[:, :4]], axis=1)

    low = iota((32, 8, 128), 1) < 4
    pairs_own = rbuf[...].astype(F32)[:, 8:].reshape(32, 2, 8, 128)
    own_rows = jnp.where(low, pairs_own[:, 0], swapped(pairs_own[:, 1]))
    pool[64:320, :] = own_rows.reshape(256, 128).astype(BF16)
    swap[0].wait_recv()
    sib.wait_recv()

    gathered = gathered + mm(s_coarse[:, 1024:], cbuf[...].reshape(1024, 128))
    gathered = gathered.astype(BF16)
    coarse = jnp.zeros((8, 512), F32)
    for t in range(4):
        coarse = coarse + mm(gathered[t * 8 : (t + 1) * 8], coarsew[t])
    coarse_own[...] = coarse
    co = [remote(coarse_own, coarse_slot.at[i], co_s.at[i], co_r.at[i], xpeers[i]) for i in range(3)]

    pairs_sib = cbuf[...].astype(F32)[:, 8:].reshape(32, 2, 8, 128)
    sib_rows = jnp.where(low, swapped(pairs_sib[:, 0]), pairs_sib[:, 1])
    pool[320:576, :] = sib_rows.reshape(256, 128).astype(BF16)
    for t in range(8):
        gsum[:, t * 128 : (t + 1) * 128] = mm(s_leaf[:, t * 640 : (t + 1) * 640], pool[...]).astype(BF16)
    swap[1].wait_recv()
    far = mm(gsum[...], leafw[...].reshape(1024, 512)).astype(BF16)
    loads["l2p"].wait()
    leafpot[...] = mm(far, l2p[...])

    loads["l2l"].wait()
    for copy in co:
        copy.wait_recv()
    coarse = coarse_own[...]
    for i in range(3):
        coarse = coarse + coarse_slot[i]
    coarse = coarse.astype(BF16)
    for o in range(8):
        down[pl.ds(o, 8, stride=8), :] = mm(coarse, l2l[o])
    pot[...] = leafpot[...] + mm(down[...].astype(BF16), l2p[mine, :])
    for j in range(4):
        pot_out[j] = pot[:, j * 128 : (j + 1) * 128].astype(BF16)
    po = [
        remote(pot_out.at[lax.rem(lvl + k, 4)], pot_slot.at[i], po_s.at[i], po_r.at[i], xpeers[i])
        for i, k in enumerate(XOFF)
    ]
    result = out_ref[...] + pot[:, mine]

    for copy in mp + ch + cw + lw + swap + halo + [sib] + co:
        copy.wait_send()
    pltpu.make_async_copy(msg.at[pl.ds(0, 63)], rbuf.at[pl.ds(0, 63)], far_s).wait()
    for copy in po:
        copy.wait_recv()
    for i in range(3):
        result = result + pot_slot[i].astype(F32)
    out_ref[...] = result
    for copy in po:
        copy.wait_send()


def local(
    charges, p2m_matrix, m2m_matrices, leaf_ops, coarse_ops, l2l_matrices, l2p_matrix, near_kernel_tiles,
    send_rows, m2l_src, m2l_op, m2l_count, coarse_src, coarse_op, near_src, neighbour_kernel_type,
):
    operands = (
        charges, p2m_matrix, m2m_matrices, leaf_ops, coarse_ops, l2l_matrices, l2p_matrix, near_kernel_tiles,
        jnp.swapaxes(send_rows, 1, 2).reshape(4, 128), m2l_src.T, m2l_op.T, m2l_count.reshape(1, 64),
        coarse_src, coarse_op, near_src.T, neighbour_kernel_type.T,
    )
    dma = pltpu.SemaphoreType.DMA
    vmem = pltpu.VMEM
    scratch = [
        vmem((64, 128), BF16), vmem((128, 512), BF16), vmem((8, 512, 128), BF16), vmem((8, 512, 128), BF16),
        vmem((512, 512), BF16), vmem((4, 512, 128), BF16),
        vmem((4, 128), I32), vmem((24, 64), I32), vmem((24, 64), I32), vmem((1, 64), I32),
        vmem((8, 24), I32), vmem((8, 24), I32), vmem((8, 64), I32), vmem((8, 64), I32),
        dma((14,)),
        vmem((64, 512), F32), vmem((4, 64, 128), F32), vmem((64, 512), BF16), vmem((3, 64, 512), BF16), vmem((128, 512), BF16),
        vmem((8, 128, 512), BF16), vmem((4, 128, 512), BF16),
        vmem((512, 64), BF16), vmem((64, 5120), BF16), vmem((32, 2048), BF16), vmem((64, 512), BF16),
        vmem((64, 16, 128), BF16), vmem((64, 16, 128), BF16), vmem((64, 16, 128), BF16),
        vmem((640, 128), BF16), vmem((64, 1024), BF16),
        vmem((8, 512), F32), vmem((3, 8, 512), F32), vmem((64, 128), F32), vmem((64, 512), F32),
        vmem((64, 512), F32), vmem((4, 64, 128), BF16), vmem((3, 64, 128), BF16),
        dma((3,)), dma((3,)), dma((3,)), dma((3,)), dma((3,)), dma((3,)), dma((3,)), dma((3,)),
        dma((2,)), dma((2,)), dma((2,)), dma((2,)), dma((2,)),
        dma, dma, dma, dma, dma((3,)), dma((3,)), dma((3,)), dma((3,)),
        pltpu.SemaphoreType.REGULAR,
    ]
    return pl.pallas_call(
        kernel,
        out_shape=jax.ShapeDtypeStruct((64, 128), F32),
        in_specs=[pl.BlockSpec(memory_space=pl.ANY)] * len(operands),
        out_specs=pl.BlockSpec(memory_space=pltpu.VMEM),
        scratch_shapes=scratch,
        compiler_params=pltpu.CompilerParams(
            collective_id=0, has_side_effects=True, vmem_limit_bytes=60 * 2**20
        ),
    )(*operands)


def solution(mesh):
    placed = (
        P("leaf", "lvl"),
        P("lvl", None),
        P(None, None, "lvl"),
        P(None, None, "lvl"),
        P(None, None, "lvl"),
        P(None, None, "lvl"),
        P(),
        P(None, None, "lvl"),
        P("leaf", None, None),
        P("leaf", None),
        P("leaf", None),
        P("leaf"),
        P("leaf", None),
        P("leaf", None),
        P("leaf", None),
        P("leaf", None),
    )
    return jax.shard_map(
        local, mesh=mesh, in_specs=placed, out_specs=P("leaf", "lvl"), check_vma=False
    )
```

```python
import jax
import jax.numpy as jnp
from jax import lax
from jax.experimental import pallas as pl
from jax.experimental.pallas import tpu as pltpu
from jax.sharding import PartitionSpec as P

MESH = pl.DeviceIdType.MESH
BF16 = jnp.bfloat16
F32 = jnp.float32
I32 = jnp.int32
XOFF = (2, 1, 3)


def mm(a, b):
    return jnp.dot(a, b, preferred_element_type=F32)


def mm_nt(a, b):
    return lax.dot_general(a, b, (((1,), (1,)), ((), ())), preferred_element_type=F32)


def iota(shape, dim):
    return lax.broadcasted_iota(I32, shape, dim)


def flipped(code):
    slots, leaves = code.shape
    halves = jnp.concatenate([code >> 6, code & 63], axis=0).astype(F32).astype(BF16)
    eye = (iota((leaves, leaves), 0) == iota((leaves, leaves), 1)).astype(F32).astype(BF16)
    turned = mm_nt(eye, halves)
    return (turned[:, :slots] * 64.0 + turned[:, slots:]).astype(I32)


def counts(code, width, start):
    rows, slots = code.shape
    columns = iota((rows, width), 1)
    code = code - start
    total = jnp.zeros((rows, width), F32)
    for s in range(slots):
        total = total + jnp.where(code[:, s : s + 1] == columns, 1.0, 0.0)
    return total.astype(BF16)


def kernel(
    charges_h, p2m_h, m2m_h, lops_h, cops_h, l2l_h, l2p_h, tiles_h,
    send_h, src_h, op_h, count_h, csrc_h, cop_h, near_h, kind_h,
    out_ref,
    charges, p2m, m2m, l2l, l2p, tiles,
    send, src, op, count, cells, near_v, kind_v,
    load_sem,
    mom32, mom4, mpart, mslot, ext, leafw, coarsew,
    pick, s_leaf, s_coarse, s_near,
    msg, rbuf, cbuf, pool,
    coarse_own, coarse_slot, down, leafpot, pot, pot_out, pot_slot,
    mp_s, mp_r, ch_s, ch_r, lw_s, lw_r, cw_s, cw_r, own_w, sw_s, sw_r,
    halo_s, halo_r, far_s, far_r, sib_s, sib_r, co_s, co_r, po_s, po_r,
    ct_s, ct_r, ready,
):
    leaf = lax.axis_index("leaf")
    lvl = lax.axis_index("lvl")
    core = lax.rem(leaf, 2)
    chip = lax.div(leaf, 2)
    z = lax.div(leaf, 16)
    y = lax.rem(chip, 8)
    other = 1 - core
    sibling = (chip * 2 + other, lvl)
    right = (lax.rem(leaf + 1, 128), lvl)
    left = (lax.rem(leaf + 127, 128), lvl)
    beside = (lax.rem(leaf + 127 + 2 * core, 128), lvl)
    near_far = (4, 3, 5, 2, 6, 1, 7)
    zpeers = [(lax.rem(z + k, 8) * 16 + y * 2 + core, lvl) for k in near_far]
    ypeers = [(z * 16 + lax.rem(y + k, 8) * 2 + core, lvl) for k in near_far]
    xpeers = [(leaf, lax.rem(lvl + k, 4)) for k in XOFF]
    across = [(chip * 2 + other, lax.rem(lvl + k, 4)) for k in XOFF]
    mine = pl.ds(pl.multiple_of(lvl * 128, 128), 128)

    barrier = pltpu.get_barrier_semaphore()
    greeted = zpeers + ypeers + xpeers + across + [sibling, beside]
    for peer in greeted:
        pl.semaphore_signal(barrier, inc=1, device_id=peer, device_id_type=MESH)

    loads = {}
    pairs = (
        ("charges", charges_h, charges), ("p2m", p2m_h, p2m), ("send", send_h, send),
        ("csrc", csrc_h, cells.at[0, 0]), ("cop", cop_h, cells.at[0, 1]), ("near", near_h, near_v), ("kind", kind_h, kind_v),
        ("src", src_h, src), ("op", op_h, op), ("count", count_h, count),
        ("m2m", m2m_h, m2m), ("tiles", tiles_h, tiles), ("l2l", l2l_h, l2l), ("l2p", l2p_h, l2p),
    )
    for i, (name, source, target) in enumerate(pairs):
        loads[name] = pltpu.make_async_copy(source, target, load_sem.at[i])
        loads[name].start()

    def remote(source, target, send_sem, recv_sem, peer):
        copy = pltpu.make_async_remote_copy(
            src_ref=source, dst_ref=target, send_sem=send_sem, recv_sem=recv_sem,
            device_id=peer, device_id_type=MESH,
        )
        copy.start()
        return copy

    loads["charges"].wait()
    loads["p2m"].wait()
    partial = mm(charges[...], p2m[...])
    mom32[...] = partial
    mpart[...] = partial.astype(BF16)
    ext[32:96, mine] = charges[...]

    pl.semaphore_wait(barrier, len(greeted))

    mp = [remote(mpart, mslot.at[i], mp_s.at[i], mp_r.at[i], xpeers[i]) for i in range(3)]
    ch = [
        remote(charges, ext.at[pl.ds(32, 64), mine], ch_s.at[i], ch_r.at[i], xpeers[i])
        for i in range(3)
    ]
    loads["csrc"].wait()
    loads["cop"].wait()
    ct = [remote(cells.at[0], cells.at[1], ct_s, ct_r, sibling)]
    for peer in ypeers:
        pl.semaphore_signal(ready, inc=1, device_id=peer, device_id_type=MESH)

    loads["send"].wait()
    row = iota((512, 128), 0)
    dest = (row >> 3) * 2 + jnp.where(((row >> 2) & 1) == 0, core, other)
    spread = (dest == iota((512, 128), 1)).astype(F32).astype(BF16)
    chosen = mm_nt(spread, send[...].astype(F32).astype(BF16))
    slot = iota((512, 4), 1) == (iota((512, 4), 0) & 3)
    chosen = jnp.sum(jnp.where(slot, chosen, 0.0), axis=1, keepdims=True).astype(I32)
    pick[...] = (chosen == iota((512, 64), 1)).astype(F32).astype(BF16)

    loads["src"].wait()
    loads["op"].wait()
    loads["count"].wait()
    sv = src[...]
    w = sv - 64
    sent = ((w >> 3) << 2) + (w & 3) + jnp.where(((w >> 2) & 1) == core, 0, 256)
    spos = jnp.where(sv < 64, sv + 512, sent)
    scode = jnp.where(iota((24, 64), 0) < count[...], op[...] * 640 + spos, -1)
    scode = flipped(scode)

    def fill(t, carry):
        s_leaf[pl.ds(pl.multiple_of(t * 64, 64), 64), :] = counts(scode, 640, t * 640)
        return carry

    lax.fori_loop(0, 8, fill, 0)

    for copy in mp:
        copy.wait_recv()
    moments = mom32[...]
    for i in range(3):
        moments = moments + mslot[i].astype(F32)
    moments = moments.astype(BF16).astype(F32)
    for j in range(4):
        mom4[j] = moments[:, j * 128 : (j + 1) * 128]

    chalf = pl.ds(core * 2, 2)
    lhalf = pl.ds(core * 4, 4)
    cw, lw = [], []
    for i, k in enumerate(XOFF):
        rows = pl.ds(pl.multiple_of(lax.rem(lvl + k, 4) * 128, 128), 128)
        cw.append(remote(cops_h.at[chalf, rows], coarsew.at[chalf, :, mine], cw_s.at[i], cw_r.at[i], xpeers[i]))
    for i, k in enumerate(XOFF):
        rows = pl.ds(pl.multiple_of(lax.rem(lvl + k, 4) * 128, 128), 128)
        lw.append(remote(lops_h.at[lhalf, rows], leafw.at[lhalf, :, mine], lw_s.at[i], lw_r.at[i], xpeers[i]))
    own_c = pltpu.make_async_copy(cops_h.at[chalf, mine], coarsew.at[chalf, :, mine], own_w.at[0])
    own_l = pltpu.make_async_copy(lops_h.at[lhalf, mine], leafw.at[lhalf, :, mine], own_w.at[1])
    own_c.start()
    own_l.start()

    loads["m2m"].wait()
    parents = jnp.zeros((8, 128), F32)
    for o in range(8):
        octant = [mom4[j, pl.ds(o, 8, stride=8), :] for j in range(4)]
        parents = parents + mm(jnp.concatenate(octant, axis=1).astype(BF16), m2m[o])
    quarter = mom4[lvl].astype(BF16)
    chosen_rows = mm(pick[...], quarter).reshape(64, 8, 128)
    both = jnp.concatenate([jnp.broadcast_to(parents[None], (64, 8, 128)), chosen_rows], axis=1)
    msg[...] = both.astype(BF16)

    pl.semaphore_wait(ready, 7)

    def offset(t):
        return 4 + (1 - 2 * lax.rem(t, 2)) * lax.div(t + 1, 2)

    def send_one(i, carry):
        pz = lax.rem(z + offset(lax.div(i, 8)), 8)
        py = lax.rem(y + offset(lax.rem(i, 8)), 8)
        there = pz * 8 + py
        pltpu.make_async_remote_copy(
            src_ref=msg.at[there], dst_ref=rbuf.at[chip], send_sem=far_s, recv_sem=far_r,
            device_id=(there * 2 + core, lvl), device_id_type=MESH,
        ).start()
        return carry

    lax.fori_loop(0, 63, send_one, 0)
    rbuf[pl.ds(chip, 1)] = msg[pl.ds(chip, 1)]
    pool[512:576, :] = quarter
    pool[576:640, :] = jnp.zeros((64, 128), BF16)

    for copy in ct:
        copy.wait_recv()
    ccode = []
    for c in range(2):
        cv = cells[c, 0]
        cpos = jnp.where(((cv >> 3) & 1) == core, (cv & ~15) + (cv & 7), -1)
        ccode += [jnp.where(cells[c, 1] == t, cpos, -1) for t in range(4)]
    ccode = jnp.concatenate(ccode, axis=0)
    for part in range(2):
        s_coarse[:, part * 512 : (part + 1) * 512] = counts(ccode, 512, part * 512)

    loads["near"].wait()
    loads["kind"].wait()
    ncode = kind_v[...] * 128 + (near_v[...] - (leaf * 64 - 32))
    s_near[...] = counts(flipped(ncode), 512, 0)

    for copy in ch:
        copy.wait_recv()
    halo = [
        remote(ext.at[pl.ds(64, 32)], ext.at[pl.ds(0, 32)], halo_s.at[0], halo_r.at[0], right),
        remote(ext.at[pl.ds(32, 32)], ext.at[pl.ds(96, 32)], halo_s.at[1], halo_r.at[1], left),
    ]

    own_c.wait()
    for copy in cw:
        copy.wait_recv()
    swap = [remote(coarsew.at[chalf], coarsew.at[chalf], sw_s.at[0], sw_r.at[0], sibling)]

    for copy in halo:
        copy.wait_recv()
    loads["tiles"].wait()
    close = jnp.zeros((64, 128), F32)
    for t in range(4):
        close = close + mm(s_near[:, t * 128 : (t + 1) * 128], mm(ext[...], tiles[t]).astype(BF16))
    out_ref[...] = close

    own_l.wait()
    for copy in lw:
        copy.wait_recv()
    swap.append(remote(leafw.at[lhalf], leafw.at[lhalf], sw_s.at[1], sw_r.at[1], sibling))

    pltpu.make_async_copy(msg.at[pl.ds(0, 63)], rbuf.at[pl.ds(0, 63)], far_r).wait()
    sib = remote(rbuf, cbuf, sib_s, sib_r, sibling)
    gathered = mm(s_coarse[...], rbuf[...].reshape(1024, 128)).astype(BF16)
    swap[0].wait_recv()
    coarse = jnp.zeros((16, 512), F32)
    for t in range(4):
        rows = jnp.concatenate([gathered[t * 8 : t * 8 + 8], gathered[32 + t * 8 : 40 + t * 8]], axis=0)
        coarse = coarse + mm(rows, coarsew[t])
    coarse_own[...] = coarse.reshape(2, 8, 512)
    co = [remote(coarse_own.at[0], coarse_slot.at[i], co_s.at[i], co_r.at[i], xpeers[i]) for i in range(3)]
    co += [remote(coarse_own.at[1], coarse_slot.at[3 + i], co_s.at[3 + i], co_r.at[3 + i], across[i]) for i in range(3)]
    co += [remote(coarse_own.at[1], coarse_slot.at[6], co_s.at[6], co_r.at[6], sibling)]

    def swapped(x):
        return jnp.concatenate([x[:, 4:], x[:, :4]], axis=1)

    low = iota((32, 8, 128), 1) < 4
    pairs_own = rbuf[...].astype(F32)[:, 8:].reshape(32, 2, 8, 128)
    own_rows = jnp.where(low, pairs_own[:, 0], swapped(pairs_own[:, 1]))
    pool[0:256, :] = own_rows.reshape(256, 128).astype(BF16)
    picked = mm(s_leaf[:, 0:256], pool[0:256, :]) + mm(s_leaf[:, 512:640], pool[512:640, :])
    sib.wait_recv()

    pairs_sib = cbuf[...].astype(F32)[:, 8:].reshape(32, 2, 8, 128)
    sib_rows = jnp.where(low, swapped(pairs_sib[:, 0]), pairs_sib[:, 1])
    pool[256:512, :] = sib_rows.reshape(256, 128).astype(BF16)
    picked = (picked + mm(s_leaf[:, 256:512], pool[256:512, :])).astype(BF16)
    picked = jnp.concatenate([picked[t * 64 : (t + 1) * 64] for t in range(8)], axis=1)
    swap[1].wait_recv()
    far = mm(picked, leafw[...].reshape(1024, 512)).astype(BF16)
    loads["l2p"].wait()
    leafpot[...] = mm(far, l2p[...])

    loads["l2l"].wait()
    for copy in co:
        copy.wait_recv()
    coarse = coarse_own[0]
    for i in range(7):
        coarse = coarse + coarse_slot[i]
    coarse = coarse.astype(BF16)
    for o in range(8):
        down[pl.ds(o, 8, stride=8), :] = mm(coarse, l2l[o])
    pot[...] = leafpot[...] + mm(down[...].astype(BF16), l2p[mine, :])
    for j in range(4):
        pot_out[j] = pot[:, j * 128 : (j + 1) * 128].astype(BF16)
    po = [
        remote(pot_out.at[lax.rem(lvl + k, 4)], pot_slot.at[i], po_s.at[i], po_r.at[i], xpeers[i])
        for i, k in enumerate(XOFF)
    ]
    result = out_ref[...] + pot[:, mine]

    for copy in ct + mp + ch + cw + lw + swap + halo + [sib] + co:
        copy.wait_send()
    pltpu.make_async_copy(msg.at[pl.ds(0, 63)], rbuf.at[pl.ds(0, 63)], far_s).wait()
    for copy in po:
        copy.wait_recv()
    for i in range(3):
        result = result + pot_slot[i].astype(F32)
    out_ref[...] = result
    for copy in po:
        copy.wait_send()


def local(
    charges, p2m_matrix, m2m_matrices, leaf_ops, coarse_ops, l2l_matrices, l2p_matrix, near_kernel_tiles,
    send_rows, m2l_src, m2l_op, m2l_count, coarse_src, coarse_op, near_src, neighbour_kernel_type,
):
    operands = (
        charges, p2m_matrix, m2m_matrices, leaf_ops, coarse_ops, l2l_matrices, l2p_matrix, near_kernel_tiles,
        jnp.swapaxes(send_rows, 1, 2).reshape(4, 128), m2l_src.T, m2l_op.T, m2l_count.reshape(1, 64),
        coarse_src, coarse_op, near_src.T, neighbour_kernel_type.T,
    )
    dma = pltpu.SemaphoreType.DMA
    vmem = pltpu.VMEM
    scratch = [
        vmem((64, 128), BF16), vmem((128, 512), BF16), vmem((8, 512, 128), BF16), vmem((8, 512, 128), BF16),
        vmem((512, 512), BF16), vmem((4, 512, 128), BF16),
        vmem((4, 128), I32), vmem((24, 64), I32), vmem((24, 64), I32), vmem((1, 64), I32),
        vmem((2, 2, 8, 24), I32), vmem((8, 64), I32), vmem((8, 64), I32),
        dma((14,)),
        vmem((64, 512), F32), vmem((4, 64, 128), F32), vmem((64, 512), BF16), vmem((3, 64, 512), BF16), vmem((128, 512), BF16),
        vmem((8, 128, 512), BF16), vmem((4, 128, 512), BF16),
        vmem((512, 64), BF16), vmem((512, 640), BF16), vmem((64, 1024), BF16), vmem((64, 512), BF16),
        vmem((64, 16, 128), BF16), vmem((64, 16, 128), BF16), vmem((64, 16, 128), BF16),
        vmem((640, 128), BF16),
        vmem((2, 8, 512), F32), vmem((7, 8, 512), F32), vmem((64, 128), F32), vmem((64, 512), F32),
        vmem((64, 512), F32), vmem((4, 64, 128), BF16), vmem((3, 64, 128), BF16),
        dma((3,)), dma((3,)), dma((3,)), dma((3,)), dma((3,)), dma((3,)), dma((3,)), dma((3,)),
        dma((2,)), dma((2,)), dma((2,)), dma((2,)), dma((2,)),
        dma, dma, dma, dma, dma((7,)), dma((7,)), dma((3,)), dma((3,)),
        dma, dma, pltpu.SemaphoreType.REGULAR,
    ]
    return pl.pallas_call(
        kernel,
        out_shape=jax.ShapeDtypeStruct((64, 128), F32),
        in_specs=[pl.BlockSpec(memory_space=pl.ANY)] * len(operands),
        out_specs=pl.BlockSpec(memory_space=pltpu.VMEM),
        scratch_shapes=scratch,
        compiler_params=pltpu.CompilerParams(
            collective_id=0, has_side_effects=True, vmem_limit_bytes=60 * 2**20
        ),
    )(*operands)


def solution(mesh):
    placed = (
        P("leaf", "lvl"),
        P("lvl", None),
        P(None, None, "lvl"),
        P(None, None, "lvl"),
        P(None, None, "lvl"),
        P(None, None, "lvl"),
        P(),
        P(None, None, "lvl"),
        P("leaf", None, None),
        P("leaf", None),
        P("leaf", None),
        P("leaf"),
        P("leaf", None),
        P("leaf", None),
        P("leaf", None),
        P("leaf", None),
    )
    return jax.shard_map(
        local, mesh=mesh, in_specs=placed, out_specs=P("leaf", "lvl"), check_vma=False
    )
```

```python
import jax
import jax.numpy as jnp
from jax import lax
from jax.experimental import pallas as pl
from jax.experimental.pallas import tpu as pltpu
from jax.sharding import PartitionSpec as P

MESH = pl.DeviceIdType.MESH
BF16 = jnp.bfloat16
F32 = jnp.float32
I32 = jnp.int32
XOFF = (2, 1, 3)


def mm(a, b):
    return jnp.dot(a, b, preferred_element_type=F32)


def mm_nt(a, b):
    return lax.dot_general(a, b, (((1,), (1,)), ((), ())), preferred_element_type=F32)


def iota(shape, dim):
    return lax.broadcasted_iota(I32, shape, dim)


def flipped(code):
    slots, leaves = code.shape
    halves = jnp.concatenate([code >> 6, code & 63], axis=0).astype(F32).astype(BF16)
    eye = (iota((leaves, leaves), 0) == iota((leaves, leaves), 1)).astype(F32).astype(BF16)
    turned = mm_nt(eye, halves)
    return (turned[:, :slots] * 64.0 + turned[:, slots:]).astype(I32)


def counts(code, width, start):
    rows, slots = code.shape
    columns = iota((rows, width), 1)
    code = code - start
    total = jnp.zeros((rows, width), F32)
    for s in range(slots):
        total = total + jnp.where(code[:, s : s + 1] == columns, 1.0, 0.0)
    return total.astype(BF16)


def kernel(
    charges_h, p2m_h, m2m_h, lops_h, cops_h, l2l_h, l2p_h, tiles_h,
    send_h, src_h, op_h, count_h, csrc_h, cop_h, near_h, kind_h,
    out_ref,
    charges, p2m, m2m, l2l, l2p, tiles,
    send, src, op, count, cells, near_v, kind_v,
    load_sem,
    mom32, mom4, mpart, mslot, ext, leafw, coarsew,
    pick, s_leaf, s_coarse, s_near,
    msg, rbuf, cbuf, pool,
    coarse_own, coarse_slot, down, leafpot, pot, pot_out, pot_slot,
    mp_s, mp_r, ch_s, ch_r, lw_s, lw_r, cw_s, cw_r, own_w, sw_s, sw_r,
    halo_s, halo_r, far_s, far_r, sib_s, sib_r, co_s, co_r, po_s, po_r,
    ct_s, ct_r, ready,
):
    leaf = lax.axis_index("leaf")
    lvl = lax.axis_index("lvl")
    core = lax.rem(leaf, 2)
    chip = lax.div(leaf, 2)
    z = lax.div(leaf, 16)
    y = lax.rem(chip, 8)
    other = 1 - core
    sibling = (chip * 2 + other, lvl)
    right = (lax.rem(leaf + 1, 128), lvl)
    left = (lax.rem(leaf + 127, 128), lvl)
    near_far = (4, 3, 5, 2, 6, 1, 7)
    zpeers = [(lax.rem(z + k, 8) * 16 + y * 2 + core, lvl) for k in near_far]
    ypeers = [(z * 16 + lax.rem(y + k, 8) * 2 + core, lvl) for k in near_far]
    xpeers = [(leaf, lax.rem(lvl + k, 4)) for k in XOFF]
    across = [(chip * 2 + other, lax.rem(lvl + k, 4)) for k in XOFF]
    mine = pl.ds(pl.multiple_of(lvl * 128, 128), 128)

    barrier = pltpu.get_barrier_semaphore()
    greeted = zpeers + ypeers + xpeers + [sibling]
    for peer in greeted:
        pl.semaphore_signal(barrier, inc=1, device_id=peer, device_id_type=MESH)

    loads = {}
    pairs = (
        ("charges", charges_h, charges), ("p2m", p2m_h, p2m), ("send", send_h, send),
        ("csrc", csrc_h, cells.at[0, 0]), ("cop", cop_h, cells.at[0, 1]), ("near", near_h, near_v), ("kind", kind_h, kind_v),
        ("src", src_h, src), ("op", op_h, op), ("count", count_h, count),
        ("m2m", m2m_h, m2m), ("tiles", tiles_h, tiles), ("l2l", l2l_h, l2l), ("l2p", l2p_h, l2p),
    )
    for i, (name, source, target) in enumerate(pairs):
        loads[name] = pltpu.make_async_copy(source, target, load_sem.at[i])
        loads[name].start()

    def remote(source, target, send_sem, recv_sem, peer):
        copy = pltpu.make_async_remote_copy(
            src_ref=source, dst_ref=target, send_sem=send_sem, recv_sem=recv_sem,
            device_id=peer, device_id_type=MESH,
        )
        copy.start()
        return copy

    loads["charges"].wait()
    loads["p2m"].wait()
    partial = mm(charges[...], p2m[...])
    mom32[...] = partial
    mpart[...] = partial.astype(BF16)
    ext[32:96, mine] = charges[...]

    pl.semaphore_wait(barrier, len(greeted))

    mp = [remote(mpart, mslot.at[i], mp_s.at[i], mp_r.at[i], xpeers[i]) for i in range(3)]
    ch = [
        remote(charges, ext.at[pl.ds(32, 64), mine], ch_s.at[i], ch_r.at[i], xpeers[i])
        for i in range(3)
    ]
    loads["csrc"].wait()
    loads["cop"].wait()
    ct = [remote(cells.at[0], cells.at[1], ct_s, ct_r, sibling)]
    for peer in ypeers:
        pl.semaphore_signal(ready, inc=1, device_id=peer, device_id_type=MESH)

    loads["send"].wait()
    row = iota((512, 128), 0)
    dest = (row >> 3) * 2 + jnp.where(((row >> 2) & 1) == 0, core, other)
    spread = (dest == iota((512, 128), 1)).astype(F32).astype(BF16)
    chosen = mm_nt(spread, send[...].astype(F32).astype(BF16))
    slot = iota((512, 4), 1) == (iota((512, 4), 0) & 3)
    chosen = jnp.sum(jnp.where(slot, chosen, 0.0), axis=1, keepdims=True).astype(I32)
    pick[...] = (chosen == iota((512, 64), 1)).astype(F32).astype(BF16)

    loads["src"].wait()
    loads["op"].wait()
    loads["count"].wait()
    sv = src[...]
    w = sv - 64
    sent = ((w >> 3) << 2) + (w & 3) + jnp.where(((w >> 2) & 1) == core, 0, 256)
    spos = jnp.where(sv < 64, sv + 512, sent)
    scode = jnp.where(iota((24, 64), 0) < count[...], op[...] * 640 + spos, -1)
    scode = flipped(scode)

    def fill(t, carry):
        s_leaf[pl.ds(pl.multiple_of(t * 64, 64), 64), :] = counts(scode, 640, t * 640)
        return carry

    lax.fori_loop(0, 8, fill, 0)

    for copy in mp:
        copy.wait_recv()
    moments = mom32[...]
    for i in range(3):
        moments = moments + mslot[i].astype(F32)
    moments = moments.astype(BF16).astype(F32)
    for j in range(4):
        mom4[j] = moments[:, j * 128 : (j + 1) * 128]

    chalf = pl.ds(core * 2, 2)
    lhalf = pl.ds(core * 4, 4)
    cw, lw = [], []
    for i, k in enumerate(XOFF):
        rows = pl.ds(pl.multiple_of(lax.rem(lvl + k, 4) * 128, 128), 128)
        cw.append(remote(cops_h.at[chalf, rows], coarsew.at[chalf, :, mine], cw_s.at[i], cw_r.at[i], xpeers[i]))
    for i, k in enumerate(XOFF):
        rows = pl.ds(pl.multiple_of(lax.rem(lvl + k, 4) * 128, 128), 128)
        lw.append(remote(lops_h.at[lhalf, rows], leafw.at[lhalf, :, mine], lw_s.at[i], lw_r.at[i], xpeers[i]))
    own_c = pltpu.make_async_copy(cops_h.at[chalf, mine], coarsew.at[chalf, :, mine], own_w.at[0])
    own_l = pltpu.make_async_copy(lops_h.at[lhalf, mine], leafw.at[lhalf, :, mine], own_w.at[1])
    own_c.start()
    own_l.start()

    loads["m2m"].wait()
    parents = jnp.zeros((8, 128), F32)
    for o in range(8):
        octant = [mom4[j, pl.ds(o, 8, stride=8), :] for j in range(4)]
        parents = parents + mm(jnp.concatenate(octant, axis=1).astype(BF16), m2m[o])
    quarter = mom4[lvl].astype(BF16)
    chosen_rows = mm(pick[...], quarter).reshape(64, 8, 128)
    both = jnp.concatenate([jnp.broadcast_to(parents[None], (64, 8, 128)), chosen_rows], axis=1)
    msg[...] = both.astype(BF16)

    pl.semaphore_wait(ready, 7)

    def offset(t):
        return 4 + (1 - 2 * lax.rem(t, 2)) * lax.div(t + 1, 2)

    def send_one(i, carry):
        pz = lax.rem(z + offset(lax.div(i, 8)), 8)
        py = lax.rem(y + offset(lax.rem(i, 8)), 8)
        there = pz * 8 + py
        pltpu.make_async_remote_copy(
            src_ref=msg.at[there], dst_ref=rbuf.at[chip], send_sem=far_s, recv_sem=far_r,
            device_id=(there * 2 + core, lvl), device_id_type=MESH,
        ).start()
        return carry

    lax.fori_loop(0, 63, send_one, 0)
    rbuf[pl.ds(chip, 1)] = msg[pl.ds(chip, 1)]
    pool[512:576, :] = quarter
    pool[576:640, :] = jnp.zeros((64, 128), BF16)

    for copy in ct:
        copy.wait_recv()
    ccode = []
    for c in range(2):
        cv = cells[c, 0]
        cpos = jnp.where(((cv >> 3) & 1) == core, (cv & ~15) + (cv & 7), -1)
        ccode += [jnp.where(cells[c, 1] == t, cpos, -1) for t in range(4)]
    ccode = jnp.concatenate(ccode, axis=0)
    for part in range(2):
        s_coarse[:, part * 512 : (part + 1) * 512] = counts(ccode, 512, part * 512)

    own_c.wait()
    for copy in cw:
        copy.wait_recv()
    swap = [remote(coarsew.at[chalf], coarsew.at[chalf], sw_s.at[0], sw_r.at[0], sibling)]

    own_l.wait()
    for copy in lw:
        copy.wait_recv()
    swap.append(remote(leafw.at[lhalf], leafw.at[lhalf], sw_s.at[1], sw_r.at[1], sibling))

    pltpu.make_async_copy(msg.at[pl.ds(0, 63)], rbuf.at[pl.ds(0, 63)], far_r).wait()
    sib = remote(rbuf, cbuf, sib_s, sib_r, sibling)
    gathered = mm(s_coarse[...], rbuf[...].reshape(1024, 128)).astype(BF16)
    swap[0].wait_recv()
    coarse = jnp.zeros((16, 512), F32)
    for t in range(4):
        rows = jnp.concatenate([gathered[t * 8 : t * 8 + 8], gathered[32 + t * 8 : 40 + t * 8]], axis=0)
        coarse = coarse + mm(rows, coarsew[t])
    coarse_own[...] = coarse.reshape(2, 8, 512)
    co = [None] * 7
    for i in range(3):
        co[i] = remote(coarse_own.at[0], coarse_slot.at[i], co_s.at[i], co_r.at[i], xpeers[i])
        co[3 + i] = remote(coarse_own.at[1], coarse_slot.at[3 + i], co_s.at[3 + i], co_r.at[3 + i], across[i])
    co[6] = remote(coarse_own.at[1], coarse_slot.at[6], co_s.at[6], co_r.at[6], sibling)

    for copy in ch:
        copy.wait_recv()
    halo = [
        remote(ext.at[pl.ds(64, 32)], ext.at[pl.ds(0, 32)], halo_s.at[0], halo_r.at[0], right),
        remote(ext.at[pl.ds(32, 32)], ext.at[pl.ds(96, 32)], halo_s.at[1], halo_r.at[1], left),
    ]

    def swapped(x):
        return jnp.concatenate([x[:, 4:], x[:, :4]], axis=1)

    low = iota((32, 8, 128), 1) < 4
    pairs_own = rbuf[...].astype(F32)[:, 8:].reshape(32, 2, 8, 128)
    own_rows = jnp.where(low, pairs_own[:, 0], swapped(pairs_own[:, 1]))
    pool[0:256, :] = own_rows.reshape(256, 128).astype(BF16)
    picked = mm(s_leaf[:, 0:256], pool[0:256, :]) + mm(s_leaf[:, 512:640], pool[512:640, :])
    sib.wait_recv()

    pairs_sib = cbuf[...].astype(F32)[:, 8:].reshape(32, 2, 8, 128)
    sib_rows = jnp.where(low, swapped(pairs_sib[:, 0]), pairs_sib[:, 1])
    pool[256:512, :] = sib_rows.reshape(256, 128).astype(BF16)
    picked = (picked + mm(s_leaf[:, 256:512], pool[256:512, :])).astype(BF16)
    picked = jnp.concatenate([picked[t * 64 : (t + 1) * 64] for t in range(8)], axis=1)
    swap[1].wait_recv()
    far = mm(picked, leafw[...].reshape(1024, 512)).astype(BF16)
    loads["l2p"].wait()
    leafpot[...] = mm(far, l2p[...])

    loads["l2l"].wait()
    for copy in co:
        copy.wait_recv()
    coarse = coarse_own[0]
    for i in range(7):
        coarse = coarse + coarse_slot[i]
    coarse = coarse.astype(BF16)
    for o in range(8):
        down[pl.ds(o, 8, stride=8), :] = mm(coarse, l2l[o])
    pot[...] = leafpot[...] + mm(down[...].astype(BF16), l2p[mine, :])
    for j in range(4):
        pot_out[j] = pot[:, j * 128 : (j + 1) * 128].astype(BF16)
    po = [
        remote(pot_out.at[lax.rem(lvl + k, 4)], pot_slot.at[i], po_s.at[i], po_r.at[i], xpeers[i])
        for i, k in enumerate(XOFF)
    ]
    loads["near"].wait()
    loads["kind"].wait()
    ncode = kind_v[...] * 128 + (near_v[...] - (leaf * 64 - 32))
    s_near[...] = counts(flipped(ncode), 512, 0)

    for copy in halo:
        copy.wait_recv()
    loads["tiles"].wait()
    close = jnp.zeros((64, 128), F32)
    for t in range(4):
        close = close + mm(s_near[:, t * 128 : (t + 1) * 128], mm(ext[...], tiles[t]).astype(BF16))
    result = close + pot[:, mine]


    for copy in ct + mp + ch + cw + lw + swap + halo + [sib] + co:
        copy.wait_send()
    pltpu.make_async_copy(msg.at[pl.ds(0, 63)], rbuf.at[pl.ds(0, 63)], far_s).wait()
    for copy in po:
        copy.wait_recv()
    for i in range(3):
        result = result + pot_slot[i].astype(F32)
    out_ref[...] = result
    for copy in po:
        copy.wait_send()


def local(
    charges, p2m_matrix, m2m_matrices, leaf_ops, coarse_ops, l2l_matrices, l2p_matrix, near_kernel_tiles,
    send_rows, m2l_src, m2l_op, m2l_count, coarse_src, coarse_op, near_src, neighbour_kernel_type,
):
    operands = (
        charges, p2m_matrix, m2m_matrices, leaf_ops, coarse_ops, l2l_matrices, l2p_matrix, near_kernel_tiles,
        jnp.swapaxes(send_rows, 1, 2).reshape(4, 128), m2l_src.T, m2l_op.T, m2l_count.reshape(1, 64),
        coarse_src, coarse_op, near_src.T, neighbour_kernel_type.T,
    )
    dma = pltpu.SemaphoreType.DMA
    vmem = pltpu.VMEM
    scratch = [
        vmem((64, 128), BF16), vmem((128, 512), BF16), vmem((8, 512, 128), BF16), vmem((8, 512, 128), BF16),
        vmem((512, 512), BF16), vmem((4, 512, 128), BF16),
        vmem((4, 128), I32), vmem((24, 64), I32), vmem((24, 64), I32), vmem((1, 64), I32),
        vmem((2, 2, 8, 24), I32), vmem((8, 64), I32), vmem((8, 64), I32),
        dma((14,)),
        vmem((64, 512), F32), vmem((4, 64, 128), F32), vmem((64, 512), BF16), vmem((3, 64, 512), BF16), vmem((128, 512), BF16),
        vmem((8, 128, 512), BF16), vmem((4, 128, 512), BF16),
        vmem((512, 64), BF16), vmem((512, 640), BF16), vmem((64, 1024), BF16), vmem((64, 512), BF16),
        vmem((64, 16, 128), BF16), vmem((64, 16, 128), BF16), vmem((64, 16, 128), BF16),
        vmem((640, 128), BF16),
        vmem((2, 8, 512), F32), vmem((7, 8, 512), F32), vmem((64, 128), F32), vmem((64, 512), F32),
        vmem((64, 512), F32), vmem((4, 64, 128), BF16), vmem((3, 64, 128), BF16),
        dma((3,)), dma((3,)), dma((3,)), dma((3,)), dma((3,)), dma((3,)), dma((3,)), dma((3,)),
        dma((2,)), dma((2,)), dma((2,)), dma((2,)), dma((2,)),
        dma, dma, dma, dma, dma((7,)), dma((7,)), dma((3,)), dma((3,)),
        dma, dma, pltpu.SemaphoreType.REGULAR,
    ]
    return pl.pallas_call(
        kernel,
        out_shape=jax.ShapeDtypeStruct((64, 128), F32),
        in_specs=[pl.BlockSpec(memory_space=pl.ANY)] * len(operands),
        out_specs=pl.BlockSpec(memory_space=pltpu.VMEM),
        scratch_shapes=scratch,
        compiler_params=pltpu.CompilerParams(
            collective_id=0, has_side_effects=True, vmem_limit_bytes=60 * 2**20
        ),
    )(*operands)


def solution(mesh):
    placed = (
        P("leaf", "lvl"),
        P("lvl", None),
        P(None, None, "lvl"),
        P(None, None, "lvl"),
        P(None, None, "lvl"),
        P(None, None, "lvl"),
        P(),
        P(None, None, "lvl"),
        P("leaf", None, None),
        P("leaf", None),
        P("leaf", None),
        P("leaf"),
        P("leaf", None),
        P("leaf", None),
        P("leaf", None),
        P("leaf", None),
    )
    return jax.shard_map(
        local, mesh=mesh, in_specs=placed, out_specs=P("leaf", "lvl"), check_vma=False
    )
```

```python
import jax
import jax.numpy as jnp
from jax import lax
from jax.experimental import pallas as pl
from jax.experimental.pallas import tpu as pltpu
from jax.sharding import PartitionSpec as P

MESH = pl.DeviceIdType.MESH
BF16 = jnp.bfloat16
F32 = jnp.float32
I32 = jnp.int32
XOFF = (2, 1, 3)


def mm(a, b):
    return jnp.dot(a, b, preferred_element_type=F32)


def mm_nt(a, b):
    return lax.dot_general(a, b, (((1,), (1,)), ((), ())), preferred_element_type=F32)


def iota(shape, dim):
    return lax.broadcasted_iota(I32, shape, dim)


def flipped(code):
    slots, leaves = code.shape
    halves = jnp.concatenate([code >> 6, code & 63], axis=0).astype(F32).astype(BF16)
    eye = (iota((leaves, leaves), 0) == iota((leaves, leaves), 1)).astype(F32).astype(BF16)
    turned = mm_nt(eye, halves)
    return (turned[:, :slots] * 64.0 + turned[:, slots:]).astype(I32)


def counts(code, width, start):
    rows, slots = code.shape
    columns = iota((rows, width), 1)
    code = code - start
    total = jnp.zeros((rows, width), F32)
    for s in range(slots):
        total = total + jnp.where(code[:, s : s + 1] == columns, 1.0, 0.0)
    return total.astype(BF16)


def kernel(
    charges_h, p2m_h, m2m_h, lops_h, cops_h, l2l_h, l2p_h, tiles_h,
    send_h, src_h, op_h, count_h, csrc_h, cop_h, near_h, kind_h,
    out_ref,
    charges, p2m, m2m, l2l, l2p, tiles,
    send, src, op, count, cells, near_v, kind_v,
    load_sem,
    mom32, mom4, mpart, mslot, ext, leafw, coarsew,
    pick, s_leaf, s_coarse, s_near,
    msg, rbuf, cbuf, pool,
    coarse_own, coarse_slot, down, leafpot, pot, pot_out, pot_slot,
    mp_s, mp_r, ch_s, ch_r, lw_s, lw_r, cw_s, cw_r, own_w, sw_s, sw_r,
    halo_s, halo_r, far_s, far_r, sib_s, sib_r, co_s, co_r, po_s, po_r,
    ct_s, ct_r, ready,
):
    leaf = lax.axis_index("leaf")
    lvl = lax.axis_index("lvl")
    core = lax.rem(leaf, 2)
    chip = lax.div(leaf, 2)
    z = lax.div(leaf, 16)
    y = lax.rem(chip, 8)
    other = 1 - core
    sibling = (chip * 2 + other, lvl)
    right = (lax.rem(leaf + 1, 128), lvl)
    left = (lax.rem(leaf + 127, 128), lvl)
    near_far = (4, 3, 5, 2, 6, 1, 7)
    zpeers = [(lax.rem(z + k, 8) * 16 + y * 2 + core, lvl) for k in near_far]
    ypeers = [(z * 16 + lax.rem(y + k, 8) * 2 + core, lvl) for k in near_far]
    xpeers = [(leaf, lax.rem(lvl + k, 4)) for k in XOFF]
    across = [(chip * 2 + other, lax.rem(lvl + k, 4)) for k in XOFF]
    mine = pl.ds(pl.multiple_of(lvl * 128, 128), 128)

    barrier = pltpu.get_barrier_semaphore()
    greeted = zpeers + ypeers + xpeers + [sibling]
    for peer in greeted:
        pl.semaphore_signal(barrier, inc=1, device_id=peer, device_id_type=MESH)

    loads = {}
    pairs = (
        ("charges", charges_h, charges), ("p2m", p2m_h, p2m), ("send", send_h, send),
        ("csrc", csrc_h, cells.at[0, 0]), ("cop", cop_h, cells.at[0, 1]), ("near", near_h, near_v), ("kind", kind_h, kind_v),
        ("src", src_h, src), ("op", op_h, op), ("count", count_h, count),
        ("m2m", m2m_h, m2m), ("tiles", tiles_h, tiles), ("l2l", l2l_h, l2l), ("l2p", l2p_h, l2p),
    )
    for i, (name, source, target) in enumerate(pairs):
        loads[name] = pltpu.make_async_copy(source, target, load_sem.at[i])
        loads[name].start()

    def remote(source, target, send_sem, recv_sem, peer):
        copy = pltpu.make_async_remote_copy(
            src_ref=source, dst_ref=target, send_sem=send_sem, recv_sem=recv_sem,
            device_id=peer, device_id_type=MESH,
        )
        copy.start()
        return copy

    loads["charges"].wait()
    loads["p2m"].wait()
    partial = mm(charges[...], p2m[...])
    mom32[...] = partial
    mpart[...] = partial.astype(BF16)
    ext[32:96, mine] = charges[...]

    pl.semaphore_wait(barrier, len(greeted))

    mp = [remote(mpart, mslot.at[i], mp_s.at[i], mp_r.at[i], xpeers[i]) for i in range(3)]
    loads["csrc"].wait()
    loads["cop"].wait()
    ct = [remote(cells.at[0], cells.at[1], ct_s, ct_r, sibling)]
    for peer in ypeers:
        pl.semaphore_signal(ready, inc=1, device_id=peer, device_id_type=MESH)

    loads["send"].wait()
    row = iota((512, 128), 0)
    dest = (row >> 3) * 2 + jnp.where(((row >> 2) & 1) == 0, core, other)
    spread = (dest == iota((512, 128), 1)).astype(F32).astype(BF16)
    chosen = mm_nt(spread, send[...].astype(F32).astype(BF16))
    slot = iota((512, 4), 1) == (iota((512, 4), 0) & 3)
    chosen = jnp.sum(jnp.where(slot, chosen, 0.0), axis=1, keepdims=True).astype(I32)
    pick[...] = (chosen == iota((512, 64), 1)).astype(F32).astype(BF16)

    loads["src"].wait()
    loads["op"].wait()
    loads["count"].wait()
    sv = src[...]
    w = sv - 64
    sent = ((w >> 3) << 2) + (w & 3) + jnp.where(((w >> 2) & 1) == core, 0, 256)
    spos = jnp.where(sv < 64, sv + 512, sent)
    scode = jnp.where(iota((24, 64), 0) < count[...], op[...] * 640 + spos, -1)
    scode = flipped(scode)

    def fill(t, carry):
        s_leaf[pl.ds(pl.multiple_of(t * 64, 64), 64), :] = counts(scode, 640, t * 640)
        return carry

    lax.fori_loop(0, 8, fill, 0)

    for copy in mp:
        copy.wait_recv()
    moments = mom32[...]
    for i in range(3):
        moments = moments + mslot[i].astype(F32)
    moments = moments.astype(BF16).astype(F32)
    for j in range(4):
        mom4[j] = moments[:, j * 128 : (j + 1) * 128]

    chalf = pl.ds(core * 2, 2)
    lhalf = pl.ds(core * 4, 4)
    cw, lw = [], []
    for i, k in enumerate(XOFF):
        rows = pl.ds(pl.multiple_of(lax.rem(lvl + k, 4) * 128, 128), 128)
        cw.append(remote(cops_h.at[chalf, rows], coarsew.at[chalf, :, mine], cw_s.at[i], cw_r.at[i], xpeers[i]))
    for i, k in enumerate(XOFF):
        rows = pl.ds(pl.multiple_of(lax.rem(lvl + k, 4) * 128, 128), 128)
        lw.append(remote(lops_h.at[lhalf, rows], leafw.at[lhalf, :, mine], lw_s.at[i], lw_r.at[i], xpeers[i]))
    own_c = pltpu.make_async_copy(cops_h.at[chalf, mine], coarsew.at[chalf, :, mine], own_w.at[0])
    own_l = pltpu.make_async_copy(lops_h.at[lhalf, mine], leafw.at[lhalf, :, mine], own_w.at[1])
    own_c.start()
    own_l.start()

    loads["m2m"].wait()
    parents = jnp.zeros((8, 128), F32)
    for o in range(8):
        octant = [mom4[j, pl.ds(o, 8, stride=8), :] for j in range(4)]
        parents = parents + mm(jnp.concatenate(octant, axis=1).astype(BF16), m2m[o])
    quarter = mom4[lvl].astype(BF16)
    chosen_rows = mm(pick[...], quarter).reshape(64, 8, 128)
    both = jnp.concatenate([jnp.broadcast_to(parents[None], (64, 8, 128)), chosen_rows], axis=1)
    msg[...] = both.astype(BF16)

    pl.semaphore_wait(ready, 7)

    def offset(t):
        return 4 + (1 - 2 * lax.rem(t, 2)) * lax.div(t + 1, 2)

    def send_one(i, carry):
        pz = lax.rem(z + offset(lax.div(i, 8)), 8)
        py = lax.rem(y + offset(lax.rem(i, 8)), 8)
        there = pz * 8 + py
        pltpu.make_async_remote_copy(
            src_ref=msg.at[there], dst_ref=rbuf.at[chip], send_sem=far_s, recv_sem=far_r,
            device_id=(there * 2 + core, lvl), device_id_type=MESH,
        ).start()
        return carry

    lax.fori_loop(0, 63, send_one, 0)
    ch = [
        remote(charges, ext.at[pl.ds(32, 64), mine], ch_s.at[i], ch_r.at[i], xpeers[i])
        for i in range(3)
    ]
    rbuf[pl.ds(chip, 1)] = msg[pl.ds(chip, 1)]
    pool[512:576, :] = quarter
    pool[576:640, :] = jnp.zeros((64, 128), BF16)

    for copy in ct:
        copy.wait_recv()
    ccode = []
    for c in range(2):
        cv = cells[c, 0]
        cpos = jnp.where(((cv >> 3) & 1) == core, (cv & ~15) + (cv & 7), -1)
        ccode += [jnp.where(cells[c, 1] == t, cpos, -1) for t in range(4)]
    ccode = jnp.concatenate(ccode, axis=0)
    for part in range(2):
        s_coarse[:, part * 512 : (part + 1) * 512] = counts(ccode, 512, part * 512)

    own_c.wait()
    for copy in cw:
        copy.wait_recv()
    swap = [remote(coarsew.at[chalf], coarsew.at[chalf], sw_s.at[0], sw_r.at[0], sibling)]

    own_l.wait()
    for copy in lw:
        copy.wait_recv()
    swap.append(remote(leafw.at[lhalf], leafw.at[lhalf], sw_s.at[1], sw_r.at[1], sibling))

    pltpu.make_async_copy(msg.at[pl.ds(0, 63)], rbuf.at[pl.ds(0, 63)], far_r).wait()
    sib = remote(rbuf, cbuf, sib_s, sib_r, sibling)
    gathered = mm(s_coarse[...], rbuf[...].reshape(1024, 128)).astype(BF16)
    swap[0].wait_recv()
    coarse = jnp.zeros((16, 512), F32)
    for t in range(4):
        rows = jnp.concatenate([gathered[t * 8 : t * 8 + 8], gathered[32 + t * 8 : 40 + t * 8]], axis=0)
        coarse = coarse + mm(rows, coarsew[t])
    coarse_own[...] = coarse.reshape(2, 8, 512)
    co = [None] * 7
    for i in range(3):
        co[i] = remote(coarse_own.at[0], coarse_slot.at[i], co_s.at[i], co_r.at[i], xpeers[i])
        co[3 + i] = remote(coarse_own.at[1], coarse_slot.at[3 + i], co_s.at[3 + i], co_r.at[3 + i], across[i])
    co[6] = remote(coarse_own.at[1], coarse_slot.at[6], co_s.at[6], co_r.at[6], sibling)

    for copy in ch:
        copy.wait_recv()
    halo = [
        remote(ext.at[pl.ds(64, 32)], ext.at[pl.ds(0, 32)], halo_s.at[0], halo_r.at[0], right),
        remote(ext.at[pl.ds(32, 32)], ext.at[pl.ds(96, 32)], halo_s.at[1], halo_r.at[1], left),
    ]

    def swapped(x):
        return jnp.concatenate([x[:, 4:], x[:, :4]], axis=1)

    low = iota((32, 8, 128), 1) < 4
    pairs_own = rbuf[...].astype(F32)[:, 8:].reshape(32, 2, 8, 128)
    own_rows = jnp.where(low, pairs_own[:, 0], swapped(pairs_own[:, 1]))
    pool[0:256, :] = own_rows.reshape(256, 128).astype(BF16)
    picked = mm(s_leaf[:, 0:256], pool[0:256, :]) + mm(s_leaf[:, 512:640], pool[512:640, :])
    sib.wait_recv()

    pairs_sib = cbuf[...].astype(F32)[:, 8:].reshape(32, 2, 8, 128)
    sib_rows = jnp.where(low, swapped(pairs_sib[:, 0]), pairs_sib[:, 1])
    pool[256:512, :] = sib_rows.reshape(256, 128).astype(BF16)
    picked = (picked + mm(s_leaf[:, 256:512], pool[256:512, :])).astype(BF16)
    picked = jnp.concatenate([picked[t * 64 : (t + 1) * 64] for t in range(8)], axis=1)
    swap[1].wait_recv()
    far = mm(picked, leafw[...].reshape(1024, 512)).astype(BF16)
    loads["l2p"].wait()
    leafpot[...] = mm(far, l2p[...])

    loads["l2l"].wait()
    for copy in co:
        copy.wait_recv()
    coarse = coarse_own[0]
    for i in range(7):
        coarse = coarse + coarse_slot[i]
    coarse = coarse.astype(BF16)
    for o in range(8):
        down[pl.ds(o, 8, stride=8), :] = mm(coarse, l2l[o])
    pot[...] = leafpot[...] + mm(down[...].astype(BF16), l2p[mine, :])
    for j in range(4):
        pot_out[j] = pot[:, j * 128 : (j + 1) * 128].astype(BF16)
    po = [
        remote(pot_out.at[lax.rem(lvl + k, 4)], pot_slot.at[i], po_s.at[i], po_r.at[i], xpeers[i])
        for i, k in enumerate(XOFF)
    ]
    loads["near"].wait()
    loads["kind"].wait()
    ncode = kind_v[...] * 128 + (near_v[...] - (leaf * 64 - 32))
    s_near[...] = counts(flipped(ncode), 512, 0)

    for copy in halo:
        copy.wait_recv()
    loads["tiles"].wait()
    close = jnp.zeros((64, 128), F32)
    for t in range(4):
        close = close + mm(s_near[:, t * 128 : (t + 1) * 128], mm(ext[...], tiles[t]).astype(BF16))
    result = close + pot[:, mine]


    for copy in ct + mp + ch + cw + lw + swap + halo + [sib] + co:
        copy.wait_send()
    pltpu.make_async_copy(msg.at[pl.ds(0, 63)], rbuf.at[pl.ds(0, 63)], far_s).wait()
    for copy in po:
        copy.wait_recv()
    for i in range(3):
        result = result + pot_slot[i].astype(F32)
    out_ref[...] = result
    for copy in po:
        copy.wait_send()


def local(
    charges, p2m_matrix, m2m_matrices, leaf_ops, coarse_ops, l2l_matrices, l2p_matrix, near_kernel_tiles,
    send_rows, m2l_src, m2l_op, m2l_count, coarse_src, coarse_op, near_src, neighbour_kernel_type,
):
    operands = (
        charges, p2m_matrix, m2m_matrices, leaf_ops, coarse_ops, l2l_matrices, l2p_matrix, near_kernel_tiles,
        jnp.swapaxes(send_rows, 1, 2).reshape(4, 128), m2l_src.T, m2l_op.T, m2l_count.reshape(1, 64),
        coarse_src, coarse_op, near_src.T, neighbour_kernel_type.T,
    )
    dma = pltpu.SemaphoreType.DMA
    vmem = pltpu.VMEM
    scratch = [
        vmem((64, 128), BF16), vmem((128, 512), BF16), vmem((8, 512, 128), BF16), vmem((8, 512, 128), BF16),
        vmem((512, 512), BF16), vmem((4, 512, 128), BF16),
        vmem((4, 128), I32), vmem((24, 64), I32), vmem((24, 64), I32), vmem((1, 64), I32),
        vmem((2, 2, 8, 24), I32), vmem((8, 64), I32), vmem((8, 64), I32),
        dma((14,)),
        vmem((64, 512), F32), vmem((4, 64, 128), F32), vmem((64, 512), BF16), vmem((3, 64, 512), BF16), vmem((128, 512), BF16),
        vmem((8, 128, 512), BF16), vmem((4, 128, 512), BF16),
        vmem((512, 64), BF16), vmem((512, 640), BF16), vmem((64, 1024), BF16), vmem((64, 512), BF16),
        vmem((64, 16, 128), BF16), vmem((64, 16, 128), BF16), vmem((64, 16, 128), BF16),
        vmem((640, 128), BF16),
        vmem((2, 8, 512), F32), vmem((7, 8, 512), F32), vmem((64, 128), F32), vmem((64, 512), F32),
        vmem((64, 512), F32), vmem((4, 64, 128), BF16), vmem((3, 64, 128), BF16),
        dma((3,)), dma((3,)), dma((3,)), dma((3,)), dma((3,)), dma((3,)), dma((3,)), dma((3,)),
        dma((2,)), dma((2,)), dma((2,)), dma((2,)), dma((2,)),
        dma, dma, dma, dma, dma((7,)), dma((7,)), dma((3,)), dma((3,)),
        dma, dma, pltpu.SemaphoreType.REGULAR,
    ]
    return pl.pallas_call(
        kernel,
        out_shape=jax.ShapeDtypeStruct((64, 128), F32),
        in_specs=[pl.BlockSpec(memory_space=pl.ANY)] * len(operands),
        out_specs=pl.BlockSpec(memory_space=pltpu.VMEM),
        scratch_shapes=scratch,
        compiler_params=pltpu.CompilerParams(
            collective_id=0, has_side_effects=True, vmem_limit_bytes=60 * 2**20
        ),
    )(*operands)


def solution(mesh):
    placed = (
        P("leaf", "lvl"),
        P("lvl", None),
        P(None, None, "lvl"),
        P(None, None, "lvl"),
        P(None, None, "lvl"),
        P(None, None, "lvl"),
        P(),
        P(None, None, "lvl"),
        P("leaf", None, None),
        P("leaf", None),
        P("leaf", None),
        P("leaf"),
        P("leaf", None),
        P("leaf", None),
        P("leaf", None),
        P("leaf", None),
    )
    return jax.shard_map(
        local, mesh=mesh, in_specs=placed, out_specs=P("leaf", "lvl"), check_vma=False
    )
```
